32 devices in a mesh: groups: 2 (over y), row: 16 (over z, x, core).
Axes of the slice: x: 2, y: 2, z: 4, core: 2. Of those that a mesh axis runs over, the one named last changes fastest.
Arguments:
- pair: bfloat16 [32, 128, 128, 128], P(('groups', 'row')), parts along dimension 0, may hold values from -6 to 6
- comp_len: int32 [4], P('groups'), parts along dimension 0, may hold values from 129 to 384, as said below
- tile_place: int32 [32], P('groups'), parts along dimension 0, may hold values from 0 to 15, each once
- in_gain: float32 [128], replicated, may hold values from 0.1 to 1.9
- in_bias: float32 [128], replicated, may hold values from -2 to 2
- proj_weight: bfloat16 [128, 512], replicated, may hold values from -0.5 to 0.5
- gate_weight: bfloat16 [128, 128], replicated, may hold values from -0.5 to 0.5
- out_gain: float32 [128], replicated, may hold values from 0.1 to 1.9
- out_bias: float32 [128], replicated, may hold values from -2.5 to 2.5
- out_weight: bfloat16 [128, 128], replicated, may hold values from -0.5 to 0.5
Outputs:
- update: bfloat16 [32, 128, 128, 128], P(('groups', 'row')), parts along dimension 0
The draws below stay inside these ranges and needn't reach their ends.
There are 2 independent parts, one for each index of `groups`. The reference program is written for one: setup_inputs(seed, part) draws one part's arguments, and reference() takes and returns one part's arrays. A program takes and returns all parts, laid end to end along the dimension named above; an argument that names none is the same for every part. Nothing has to cross between parts.
Inputs may be any that keep to these rules, and one draw needn't show every extreme that they name: `comp_len`: complex 0 holds exactly 384 tokens; complex 1 holds more than 128 tokens, and the tiles of both complexes together fit into 16 slots. `tile_place`: A permutation of the 16 slots.
All inputs are finite; a program needn't handle non-finite values.
Results may differ from the reference program's by a relative error of at most 0.0061.
Values may be sent and summed in bfloat16 or wider, within the bound.
A program may use at most 128 MiB of HBM per device.

```python
import math
import jax
import jax.numpy as jnp
from jax import lax

CZ = 128
CH = 128
TT = 128
TILES = 16
NMAX = 3


def draw_comp_len(key, part):
    key = jax.random.fold_in(key, 11)
    first_key, second_key = jax.random.split(key)
    spare = TILES - NMAX * NMAX
    second_most = math.isqrt(spare)
    second_tiles = jax.random.randint(first_key, (), 2, second_most + 1, dtype=jnp.int32)
    second_length = (second_tiles - 1) * TT + jax.random.randint(second_key, (), 1, TT + 1, dtype=jnp.int32)
    return jnp.stack([jnp.array(NMAX * TT, jnp.int32), second_length.astype(jnp.int32)])


def block_scale(rng, dims, cuts, smallest, largest):
    def one(position, shards_of):
        steps = jax.random.uniform(jax.random.fold_in(jax.random.fold_in(rng, 6), position), (shards_of,), jnp.float32, smallest / len(cuts), largest / len(cuts))
        return jnp.repeat(jnp.exp(steps), dims[position] // shards_of).reshape((-1,) + (1,) * (len(dims) - position - 1))

    level = one(*cuts[0])
    for cut in cuts[1:]:
        level = level * one(*cut)
    return level


def noise(rng, dims, width, reach, cuts=(), held_as=jnp.bfloat16):
    values = width * jax.random.normal(rng, dims, jnp.float32)
    if cuts:
        values = values * block_scale(rng, dims, cuts, -0.22, 0.18)
    return jnp.clip(values, -reach, reach).astype(held_as)


def setup_inputs(seed: int = 0, part: int = 0) -> dict:
    keys = jax.random.split(jax.random.key(seed), 11)
    part_splits = jax.random.split(jax.random.fold_in(keys[10], part), 11)
    return {
        "pair": noise(part_splits[0], (TILES, TT, TT, CZ), 1.0, 6.0, ((0, 16),)),
        "comp_len": draw_comp_len(jax.random.fold_in(jax.random.fold_in(keys[10], part), 71), part),
        "tile_place": jax.random.permutation(part_splits[2], TILES).astype(jnp.int32),
        "in_gain": jnp.clip(1.0 + 0.18 * jax.random.normal(keys[3], (CZ,), jnp.float32), 0.1, 1.9),
        "in_bias": noise(keys[4], (CZ,), 0.4, 2.0, (), jnp.float32),
        "proj_weight": noise(keys[5], (CZ, 4 * CH), CZ ** -0.5, 0.5),
        "gate_weight": noise(keys[6], (CZ, CZ), CZ ** -0.5, 0.5),
        "out_gain": jnp.clip(1.0 + 0.18 * jax.random.normal(keys[7], (CH,), jnp.float32), 0.1, 1.9),
        "out_bias": noise(keys[8], (CH,), 0.5, 2.5, (), jnp.float32),
        "out_weight": noise(keys[9], (CH, CZ), CH ** -0.5, 0.5),
    }


def pick_slot(onehot, values):
    return lax.optimization_barrier(jnp.sum(jnp.where(onehot, values[None, :], 0), 1)).astype(jnp.int32)

def tile_tables(comp_len, tile_place, tiles, tile_side, most_tiles):
    counts = ((comp_len + tile_side - 1) // tile_side).astype(jnp.int32)
    areas = (counts * counts).astype(jnp.int32)
    starts = (jnp.cumsum(areas) - areas).astype(jnp.int32)
    numbers = jnp.arange(tiles, dtype=jnp.int32)
    inside = ((numbers[:, None] >= starts[None, :]) & (numbers[:, None] < (starts + areas)[None, :])).astype(jnp.int32)
    used = lax.optimization_barrier(jnp.sum(inside, 1)).astype(jnp.int32)
    sides = lax.optimization_barrier(jnp.sum(inside * counts[None, :], 1)).astype(jnp.int32)
    firsts = lax.optimization_barrier(jnp.sum(inside * starts[None, :], 1)).astype(jnp.int32)
    lengths = lax.optimization_barrier(jnp.sum(inside * comp_len[None, :], 1)).astype(jnp.int32)
    local_number = numbers - firsts
    safe_side = jnp.maximum(sides, 1)
    tile_row = (local_number // safe_side).astype(jnp.int32)
    tile_col = (local_number % safe_side).astype(jnp.int32)
    onehot = tile_place[None, :] == numbers[:, None]
    slot_used = pick_slot(onehot, used)
    slot_side = pick_slot(onehot, sides)
    slot_first = pick_slot(onehot, firsts)
    slot_length = pick_slot(onehot, lengths)
    slot_row = pick_slot(onehot, tile_row)
    slot_col = pick_slot(onehot, tile_col)
    steps_k = jnp.arange(most_tiles, dtype=jnp.int32)
    left_number = jnp.clip(slot_first[:, None] + slot_row[:, None] * slot_side[:, None] + steps_k[None, :], 0, tiles - 1)
    right_number = jnp.clip(slot_first[:, None] + slot_col[:, None] * slot_side[:, None] + steps_k[None, :], 0, tiles - 1)
    left_slot = lax.optimization_barrier(jnp.sum(jnp.where(left_number[:, :, None] == numbers[None, None, :], tile_place[None, None, :], 0), 2)).astype(jnp.int32)
    right_slot = lax.optimization_barrier(jnp.sum(jnp.where(right_number[:, :, None] == numbers[None, None, :], tile_place[None, None, :], 0), 2)).astype(jnp.int32)
    valid = ((steps_k[None, :] < slot_side[:, None]) & (slot_used[:, None] > 0)).astype(jnp.float32)
    tokens = jnp.arange(tile_side, dtype=jnp.int32)
    row_ok = ((slot_row[:, None] * tile_side + tokens[None, :] < slot_length[:, None]) & (slot_used[:, None] > 0)).astype(jnp.float32)
    col_ok = ((slot_col[:, None] * tile_side + tokens[None, :] < slot_length[:, None]) & (slot_used[:, None] > 0)).astype(jnp.float32)
    return (left_slot, right_slot, valid, row_ok, col_ok)

def layer_norm_last(values, gain, offset):
    average = lax.optimization_barrier(jnp.mean(values, -1, keepdims=True))
    centred = values - average
    variance = lax.optimization_barrier(jnp.mean(centred * centred, -1, keepdims=True))
    return centred * lax.rsqrt(variance + 1e-05) * gain + offset

def reference(pair, comp_len, tile_place, in_gain, in_bias, proj_weight, gate_weight, out_gain, out_bias, out_weight):
    left_slot, right_slot, valid, row_ok, col_ok = tile_tables(comp_len, tile_place, TILES, TT, NMAX)

    def normalize(tile):
        flattened = tile.reshape(TT * TT, CZ).astype(jnp.float32)
        return layer_norm_last(flattened, in_gain, in_bias).astype(jnp.bfloat16)

    def project(inputs):
        tile, rows_live, cols_live = inputs
        normed = normalize(tile)
        pair_mask = (rows_live[:, None] * cols_live[None, :]).reshape(TT * TT, 1)
        projected = jnp.dot(normed, proj_weight, preferred_element_type=jnp.float32)
        left = pair_mask * jax.nn.sigmoid(projected[:, :CH]) * projected[:, CH:2 * CH]
        right = pair_mask * jax.nn.sigmoid(projected[:, 2 * CH:3 * CH]) * projected[:, 3 * CH:]
        return (left.astype(jnp.bfloat16).reshape(TT, TT, CH), right.astype(jnp.bfloat16).reshape(TT, TT, CH))
    lefts, rights = lax.map(project, (pair, row_ok, col_ok))

    def finish(inputs):
        tile, left_list, right_list, weights = inputs
        picked_left = lefts[left_list].astype(jnp.float32) * weights[:, None, None, None]
        picked_right = rights[right_list].astype(jnp.float32)
        mixed = jnp.einsum('kiac,kjac->ijc', picked_left, picked_right).astype(jnp.bfloat16)
        mixed_norm = layer_norm_last(mixed.reshape(TT * TT, CH).astype(jnp.float32), out_gain, out_bias).astype(jnp.bfloat16)
        gating = jax.nn.sigmoid(jnp.dot(normalize(tile), gate_weight, preferred_element_type=jnp.float32))
        output = gating * jnp.dot(mixed_norm, out_weight, preferred_element_type=jnp.float32)
        return output.astype(jnp.bfloat16).reshape(TT, TT, CZ)
    return lax.map(finish, (pair, left_slot, right_slot, valid))
```

```python
import functools
import jax
import jax.numpy as jnp
from jax import lax
from jax.experimental import pallas as pl
from jax.experimental.pallas import tpu as pltpu
from jax.sharding import PartitionSpec as P

ROWS = 32


def pick_slot(onehot, values):
    return jnp.sum(jnp.where(onehot, values[None, :], 0), 1)


def tile_tables(comp_len, tile_place, tiles, tile_side, most_tiles):
    counts = (comp_len + tile_side - 1) // tile_side
    areas = counts * counts
    starts = jnp.cumsum(areas) - areas
    numbers = jnp.arange(tiles, dtype=jnp.int32)
    inside = (
        (numbers[:, None] >= starts[None, :]) & (numbers[:, None] < (starts + areas)[None, :])
    ).astype(jnp.int32)
    used = jnp.sum(inside, 1)
    sides = jnp.sum(inside * counts[None, :], 1)
    firsts = jnp.sum(inside * starts[None, :], 1)
    lengths = jnp.sum(inside * comp_len[None, :], 1)
    local_number = numbers - firsts
    safe_side = jnp.maximum(sides, 1)
    tile_row = local_number // safe_side
    tile_col = local_number % safe_side
    onehot = tile_place[None, :] == numbers[:, None]
    slot_used = pick_slot(onehot, used)
    slot_side = pick_slot(onehot, sides)
    slot_first = pick_slot(onehot, firsts)
    slot_length = pick_slot(onehot, lengths)
    slot_row = pick_slot(onehot, tile_row)
    slot_col = pick_slot(onehot, tile_col)
    steps_k = jnp.arange(most_tiles, dtype=jnp.int32)
    left_number = jnp.clip(
        slot_first[:, None] + slot_row[:, None] * slot_side[:, None] + steps_k[None, :],
        0,
        tiles - 1,
    )
    right_number = jnp.clip(
        slot_first[:, None] + slot_col[:, None] * slot_side[:, None] + steps_k[None, :],
        0,
        tiles - 1,
    )
    left_slot = jnp.sum(
        jnp.where(left_number[:, :, None] == numbers[None, None, :], tile_place[None, None, :], 0),
        2,
    )
    right_slot = jnp.sum(
        jnp.where(right_number[:, :, None] == numbers[None, None, :], tile_place[None, None, :], 0),
        2,
    )
    valid = ((steps_k[None, :] < slot_side[:, None]) & (slot_used[:, None] > 0)).astype(jnp.float32)
    own = (numbers == lax.axis_index("row")).astype(jnp.int32)
    own_length = jnp.sum(own * slot_length * slot_used)
    rows_left = own_length - jnp.sum(own * slot_row) * tile_side
    cols_left = own_length - jnp.sum(own * slot_col) * tile_side
    return (left_slot, right_slot, valid, jnp.stack([rows_left, cols_left]).astype(jnp.int32))


def kernel(
    n,
    most_tiles,
    left_slot,
    right_slot,
    valid,
    live,
    pair,
    in_gain,
    in_bias,
    proj_weight,
    gate_weight,
    out_gain,
    out_bias,
    out_weight,
    update,
    weights_t,
    gain_cols,
    bias_cols,
    stage,
    right_send,
    right_recv,
    left_send,
    mixed_send,
    mixed_recv,
    right_sems,
    left_send_sems,
    left_recv_sems,
    mixed_send_sems,
    mixed_recv_sems,
    own_sems,
    *left_recv,
):
    side = pair.shape[0]
    channels = out_weight.shape[0]
    group = channels // n
    chunks = side // ROWS
    me = lax.axis_index("row")

    barrier = pltpu.get_barrier_semaphore()

    @pl.loop(1, n)
    def _(step):
        peer = lax.rem(me + step, n)
        pl.semaphore_signal(
            barrier, inc=1, device_id={"row": peer}, device_id_type=pl.DeviceIdType.MESH
        )

    weights_t[...] = proj_weight[...].astype(jnp.float32).T.astype(jnp.bfloat16)
    gain_cols[...] = jnp.broadcast_to(out_gain[...], (side, channels)).T
    bias_cols[...] = jnp.broadcast_to(out_bias[...], (side, channels)).T

    def normalize(row):
        values = pair[row].astype(jnp.float32)
        average = jnp.mean(values, 1, keepdims=True)
        centred = values - average
        variance = jnp.mean(centred * centred, 1, keepdims=True)
        scaled = centred * lax.rsqrt(variance + 1e-05)
        return (scaled * in_gain[...] + in_bias[...]).astype(jnp.bfloat16)

    def project(which, chunk, send):
        cols = lax.broadcasted_iota(jnp.int32, (1, side), 1)
        cols_ok = (cols < live[1]).astype(jnp.float32)

        def one_row(row, carry):
            normed = normalize(chunk * ROWS + row)
            projected = lax.dot_general(
                weights_t[pl.ds(2 * which * channels, 2 * channels), :],
                normed,
                (((1,), (1,)), ((), ())),
                preferred_element_type=jnp.float32,
            )
            row_ok = (chunk * ROWS + row < live[0]).astype(jnp.float32)
            result = cols_ok * row_ok * jax.nn.sigmoid(projected[:channels]) * projected[channels:]
            stage[pl.ds(row, channels, stride=ROWS), :] = result
            return carry

        lax.fori_loop(0, ROWS, one_row, 0, unroll=2)

        def one_peer(peer, carry):
            for g in range(group):
                first = pl.multiple_of((peer * group + g) * ROWS, ROWS)
                send[peer, g, pl.ds(chunk * ROWS, ROWS), :] = stage[pl.ds(first, ROWS), :].astype(
                    jnp.bfloat16
                )
            return carry

        lax.fori_loop(0, n, one_peer, 0)

    def remote(src, dst, send_sem, recv_sem, peer):
        return pltpu.make_async_remote_copy(
            src_ref=src,
            dst_ref=dst,
            send_sem=send_sem,
            recv_sem=recv_sem,
            device_id={"row": peer},
            device_id_type=pl.DeviceIdType.MESH,
        )

    def wait_bytes(ref, sem):
        pltpu.make_async_copy(ref, ref, sem).wait()

    for chunk in range(chunks):
        rows = pl.ds(chunk * ROWS, ROWS)
        project(1, chunk, right_send)
        if chunk == 0:
            pl.semaphore_wait(barrier, n - 1)

        @pl.loop(1, n)
        def _(step):
            peer = lax.rem(me + step, n)
            remote(
                right_send.at[peer, :, rows, :],
                right_recv.at[me, :, rows, :],
                right_sems.at[0],
                right_sems.at[1],
                peer,
            ).start()

    own_right = pltpu.make_async_copy(right_send.at[me], right_recv.at[me], own_sems.at[0])
    own_right.start()

    own_left = []
    for chunk in range(chunks):
        rows = pl.ds(chunk * ROWS, ROWS)
        project(0, chunk, left_send)

        @pl.loop(1, n)
        def _(step):
            peer = lax.rem(me + step, n)
            remote(
                left_send.at[peer, :, rows, :],
                left_recv[chunk].at[me],
                left_send_sems.at[0],
                left_recv_sems.at[chunk],
                peer,
            ).start()

        copy = pltpu.make_async_copy(
            left_send.at[me, :, rows, :], left_recv[chunk].at[me], own_sems.at[1 + chunk]
        )
        copy.start()
        own_left.append(copy)

    own_right.wait()
    wait_bytes(right_recv.at[pl.ds(0, n - 1)], right_sems.at[1])

    for chunk in range(chunks):
        own_left[chunk].wait()
        wait_bytes(left_recv[chunk].at[pl.ds(0, n - 1)], left_recv_sems.at[chunk])

        def product(tile):
            for g in range(group):
                total = jnp.zeros((ROWS, side), jnp.float32)
                for k in range(most_tiles):
                    entry = tile * most_tiles + k
                    part = lax.dot_general(
                        left_recv[chunk][left_slot[entry], g],
                        right_recv[right_slot[entry], g],
                        (((1,), (1,)), ((), ())),
                        preferred_element_type=jnp.float32,
                    )
                    total = total + part * valid[entry]
                mixed_send[chunk, tile, g] = total.astype(jnp.bfloat16)

        @pl.loop(1, n)
        def _(step):
            tile = lax.rem(me + step, n)
            product(tile)
            remote(
                mixed_send.at[chunk, tile],
                mixed_recv.at[chunk, me],
                mixed_send_sems.at[0],
                mixed_recv_sems.at[chunk],
                tile,
            ).start()

        product(me)
        pltpu.make_async_copy(
            mixed_send.at[chunk, me], mixed_recv.at[chunk, me], own_sems.at[1 + chunks + chunk]
        ).start()

    for chunk in range(chunks):
        pltpu.make_async_copy(
            mixed_send.at[chunk, me], mixed_recv.at[chunk, me], own_sems.at[1 + chunks + chunk]
        ).wait()
        wait_bytes(mixed_recv.at[chunk, pl.ds(0, n - 1)], mixed_recv_sems.at[chunk])

        def unpack(source, carry):
            for g in range(group):
                first = pl.multiple_of((source * group + g) * ROWS, ROWS)
                stage[pl.ds(first, ROWS), :] = mixed_recv[chunk, source, g].astype(jnp.float32)
            return carry

        lax.fori_loop(0, n, unpack, 0)

        def finish(row, carry):
            values = stage[pl.ds(row, channels, stride=ROWS), :]
            average = jnp.mean(values, 0, keepdims=True)
            centred = values - average
            variance = jnp.mean(centred * centred, 0, keepdims=True)
            scaled = centred * lax.rsqrt(variance + 1e-05)
            mixed_norm = (scaled * gain_cols[...] + bias_cols[...]).T.astype(jnp.bfloat16)
            projected = jnp.dot(mixed_norm, out_weight[...], preferred_element_type=jnp.float32)
            normed = normalize(chunk * ROWS + row)
            gating = jax.nn.sigmoid(
                jnp.dot(normed, gate_weight[...], preferred_element_type=jnp.float32)
            )
            update[chunk * ROWS + row] = (gating * projected).astype(jnp.bfloat16)
            return carry

        lax.fori_loop(0, ROWS, finish, 0, unroll=2)

    wait_bytes(right_send.at[pl.ds(0, n - 1)], right_sems.at[0])
    wait_bytes(left_send.at[pl.ds(0, n - 1)], left_send_sems.at[0])
    wait_bytes(mixed_send.at[:, pl.ds(0, n - 1)], mixed_send_sems.at[0])


def shards(
    pair,
    comp_len,
    tile_place,
    in_gain,
    in_bias,
    proj_weight,
    gate_weight,
    out_gain,
    out_bias,
    out_weight,
):
    tiles = tile_place.shape[0]
    side = pair.shape[1]
    width = pair.shape[3]
    channels = out_weight.shape[0]
    n = lax.axis_size("row")
    group = channels // n
    most_tiles = 2 + tiles // 16
    chunks = side // ROWS
    left_slot, right_slot, valid, live = tile_tables(
        comp_len, tile_place, tiles, side, most_tiles
    )
    vmem = pl.BlockSpec(memory_space=pltpu.VMEM)
    smem = pl.BlockSpec(memory_space=pltpu.SMEM)
    result = pl.pallas_call(
        functools.partial(kernel, n, most_tiles),
        out_shape=jax.ShapeDtypeStruct((side, side, width), jnp.bfloat16),
        in_specs=[smem] * 4 + [vmem] * 8,
        out_specs=vmem,
        scratch_shapes=[
            pltpu.VMEM((4 * channels, width), jnp.bfloat16),
            pltpu.VMEM((channels, side), jnp.float32),
            pltpu.VMEM((channels, side), jnp.float32),
            pltpu.VMEM((channels * ROWS, side), jnp.float32),
            pltpu.VMEM((n, group, side, side), jnp.bfloat16),
            pltpu.VMEM((n, group, side, side), jnp.bfloat16),
            pltpu.VMEM((n, group, side, side), jnp.bfloat16),
            pltpu.VMEM((chunks, n, group, ROWS, side), jnp.bfloat16),
            pltpu.VMEM((chunks, n, group, ROWS, side), jnp.bfloat16),
            pltpu.SemaphoreType.DMA((2,)),
            pltpu.SemaphoreType.DMA((1,)),
            pltpu.SemaphoreType.DMA((chunks,)),
            pltpu.SemaphoreType.DMA((1,)),
            pltpu.SemaphoreType.DMA((chunks,)),
            pltpu.SemaphoreType.DMA((1 + 2 * chunks,)),
        ]
        + [pltpu.VMEM((n, group, ROWS, side), jnp.bfloat16)] * chunks,
        compiler_params=pltpu.CompilerParams(
            collective_id=0, has_side_effects=True, vmem_limit_bytes=56 * 1024 * 1024
        ),
    )(
        left_slot.reshape(-1),
        right_slot.reshape(-1),
        valid.reshape(-1),
        live,
        pair[0],
        in_gain[None, :],
        in_bias[None, :],
        proj_weight,
        gate_weight,
        out_gain[None, :],
        out_bias[None, :],
        out_weight,
    )
    return result[None]


def solution(mesh):
    placed = (
        P(("groups", "row"), None, None, None),
        P("groups"),
        P("groups"),
        P(),
        P(),
        P(),
        P(),
        P(),
        P(),
        P(),
    )
    return jax.shard_map(
        shards,
        mesh=mesh,
        in_specs=placed,
        out_specs=P(("groups", "row"), None, None, None),
        check_vma=False,
    )
```

```python
import functools
import jax
import jax.numpy as jnp
from jax import lax
from jax.experimental import pallas as pl
from jax.experimental.pallas import tpu as pltpu
from jax.sharding import PartitionSpec as P

RIGHT_PARTS = (16, 16, 32, 64)
LEFT_PARTS = (32, 32, 32, 16, 16)


def spans(parts):
    first = 0
    for rows in parts:
        yield (first, rows)
        first += rows


def kernel(
    n,
    most_tiles,
    comp_len,
    tile_place,
    pair_hbm,
    in_gain,
    in_bias,
    proj_weight,
    gate_weight,
    out_gain,
    out_bias,
    out_weight,
    update_hbm,
    left_slot,
    right_slot,
    valid,
    pair,
    update,
    weights_t,
    gain_cols,
    bias_cols,
    stage,
    right_send,
    right_recv,
    left_send,
    right_sems,
    left_send_sems,
    left_recv_sems,
    mixed_send_sems,
    mixed_recv_sems,
    own_sems,
    pair_sems,
    update_sems,
    *parts,
):
    chunks = len(LEFT_PARTS)
    left_recv = parts[:chunks]
    mixed_send = parts[chunks : 2 * chunks]
    mixed_recv = parts[2 * chunks :]
    side = pair.shape[0]
    channels = out_weight.shape[0]
    group = channels // n
    me = lax.axis_index("row")

    pair_copies = []
    for index, (first, rows) in enumerate(spans(RIGHT_PARTS)):
        copy = pltpu.make_async_copy(
            pair_hbm.at[pl.ds(first, rows)], pair.at[pl.ds(first, rows)], pair_sems.at[index]
        )
        copy.start()
        pair_copies.append(copy)

    barrier = pltpu.get_barrier_semaphore()

    @pl.loop(1, n)
    def _(step):
        peer = lax.rem(me + step, n)
        pl.semaphore_signal(
            barrier, inc=1, device_id={"row": peer}, device_id_type=pl.DeviceIdType.MESH
        )

    def peer_at(position):
        half = position // 2
        step = jnp.where(position % 2 == 0, n // 2 + half, half + 1)
        return lax.rem(me + step, n)

    def describe(slot):
        number = lax.fori_loop(
            0, n, lambda t, found: found + jnp.where(tile_place[t] == slot, t, 0), 0, unroll=4
        )
        start, first, count_in, length = 0, 0, 0, 0
        for c in range(comp_len.shape[0]):
            count = lax.div(comp_len[c] + (side - 1), side)
            inside = (number >= start) & (number < start + count * count)
            first = jnp.where(inside, start, first)
            count_in = jnp.where(inside, count, count_in)
            length = jnp.where(inside, comp_len[c], length)
            start = start + count * count
        local = number - first
        row = 0
        for m in range(1, most_tiles):
            row = row + jnp.where(local >= m * count_in, 1, 0)
        return first, count_in, length, row, local - row * count_in

    _, _, own_length, own_row, own_col = describe(me)
    rows_left = own_length - own_row * side
    cols_left = own_length - own_col * side

    weights_t[...] = proj_weight[...].astype(jnp.float32).T.astype(jnp.bfloat16)

    def normalize(row):
        values = pair[row].astype(jnp.float32)
        average = jnp.mean(values, 1, keepdims=True)
        centred = values - average
        variance = jnp.mean(centred * centred, 1, keepdims=True)
        scaled = centred * lax.rsqrt(variance + 1e-05)
        return (scaled * in_gain[...] + in_bias[...]).astype(jnp.bfloat16)

    def project(which, begin, rows, send):
        cols = lax.broadcasted_iota(jnp.int32, (1, side), 1)
        cols_ok = (cols < cols_left).astype(jnp.float32)

        def one_row(row, carry):
            normed = normalize(begin + row)
            projected = lax.dot_general(
                weights_t[pl.ds(2 * which * channels, 2 * channels), :],
                normed,
                (((1,), (1,)), ((), ())),
                preferred_element_type=jnp.float32,
            )
            row_ok = (begin + row < rows_left).astype(jnp.float32)
            result = cols_ok * row_ok * jax.nn.sigmoid(projected[:channels]) * projected[channels:]
            stage[pl.ds(row, channels, stride=rows), :] = result
            return carry

        lax.fori_loop(0, rows, one_row, 0, unroll=2)

        def one_peer(peer, carry):
            for g in range(group):
                first = pl.multiple_of((peer * group + g) * rows, rows)
                send[peer, g, pl.ds(begin, rows), :] = stage[pl.ds(first, rows), :].astype(
                    jnp.bfloat16
                )
            return carry

        lax.fori_loop(0, n, one_peer, 0)

    def remote(src, dst, send_sem, recv_sem, peer):
        return pltpu.make_async_remote_copy(
            src_ref=src,
            dst_ref=dst,
            send_sem=send_sem,
            recv_sem=recv_sem,
            device_id={"row": peer},
            device_id_type=pl.DeviceIdType.MESH,
        )

    def wait_bytes(ref, sem):
        pltpu.make_async_copy(ref, ref, sem).wait()

    for index, (begin, rows) in enumerate(spans(RIGHT_PARTS)):
        pair_copies[index].wait()
        project(1, begin, rows, right_send)
        if index == 0:
            pl.semaphore_wait(barrier, n - 1)

        @pl.loop(0, n - 1)
        def _(position):
            peer = peer_at(position)
            remote(
                right_send.at[peer, :, pl.ds(begin, rows), :],
                right_recv.at[me, :, pl.ds(begin, rows), :],
                right_sems.at[0],
                right_sems.at[1],
                peer,
            ).start()

    own_right = pltpu.make_async_copy(right_send.at[me], right_recv.at[me], own_sems.at[0])
    own_right.start()

    own_left = []
    for chunk, (begin, rows) in enumerate(spans(LEFT_PARTS)):
        project(0, begin, rows, left_send)

        @pl.loop(0, n - 1)
        def _(position):
            peer = peer_at(position)
            remote(
                left_send.at[peer, :, pl.ds(begin, rows), :],
                left_recv[chunk].at[me],
                left_send_sems.at[0],
                left_recv_sems.at[chunk],
                peer,
            ).start()

        copy = pltpu.make_async_copy(
            left_send.at[me, :, pl.ds(begin, rows), :],
            left_recv[chunk].at[me],
            own_sems.at[1 + chunk],
        )
        copy.start()
        own_left.append(copy)

    gain_cols[...] = jnp.broadcast_to(out_gain[...], (side, channels)).T
    bias_cols[...] = jnp.broadcast_to(out_bias[...], (side, channels)).T

    @pl.loop(0, n)
    def _(slot):
        first, count, _, row, col = describe(slot)
        for k in range(most_tiles):
            entry = slot * most_tiles + k
            left_slot[entry] = tile_place[jnp.clip(first + row * count + k, 0, n - 1)]
            right_slot[entry] = tile_place[jnp.clip(first + col * count + k, 0, n - 1)]
            valid[entry] = (k < count).astype(jnp.float32)

    own_right.wait()
    wait_bytes(right_recv.at[pl.ds(0, n - 1)], right_sems.at[1])

    own_mixed = []
    for chunk, (begin, rows) in enumerate(spans(LEFT_PARTS)):
        own_left[chunk].wait()
        wait_bytes(left_recv[chunk].at[pl.ds(0, n - 1)], left_recv_sems.at[chunk])

        def product(tile):
            for g in range(group):
                total = jnp.zeros((rows, side), jnp.float32)
                for k in range(most_tiles):
                    entry = tile * most_tiles + k
                    part = lax.dot_general(
                        left_recv[chunk][left_slot[entry], g],
                        right_recv[right_slot[entry], g],
                        (((1,), (1,)), ((), ())),
                        preferred_element_type=jnp.float32,
                    )
                    total = total + part * valid[entry]
                mixed_send[chunk][tile, g] = total.astype(jnp.bfloat16)

        @pl.loop(0, n - 1)
        def _(position):
            tile = peer_at(position)
            product(tile)
            remote(
                mixed_send[chunk].at[tile],
                mixed_recv[chunk].at[me],
                mixed_send_sems.at[chunk],
                mixed_recv_sems.at[chunk],
                tile,
            ).start()

        product(me)
        copy = pltpu.make_async_copy(
            mixed_send[chunk].at[me], mixed_recv[chunk].at[me], own_sems.at[1 + chunks + chunk]
        )
        copy.start()
        own_mixed.append(copy)

    update_copies = []
    for chunk, (begin, rows) in enumerate(spans(LEFT_PARTS)):
        own_mixed[chunk].wait()
        wait_bytes(mixed_recv[chunk].at[pl.ds(0, n - 1)], mixed_recv_sems.at[chunk])

        def unpack(source, carry):
            for g in range(group):
                first = pl.multiple_of((source * group + g) * rows, rows)
                stage[pl.ds(first, rows), :] = mixed_recv[chunk][source, g].astype(jnp.float32)
            return carry

        lax.fori_loop(0, n, unpack, 0)

        def finish(row, carry):
            values = stage[pl.ds(row, channels, stride=rows), :]
            average = jnp.mean(values, 0, keepdims=True)
            centred = values - average
            variance = jnp.mean(centred * centred, 0, keepdims=True)
            scaled = centred * lax.rsqrt(variance + 1e-05)
            mixed_norm = (scaled * gain_cols[...] + bias_cols[...]).T.astype(jnp.bfloat16)
            projected = jnp.dot(mixed_norm, out_weight[...], preferred_element_type=jnp.float32)
            normed = normalize(begin + row)
            gating = jax.nn.sigmoid(
                jnp.dot(normed, gate_weight[...], preferred_element_type=jnp.float32)
            )
            update[begin + row] = (gating * projected).astype(jnp.bfloat16)
            return carry

        lax.fori_loop(0, rows, finish, 0, unroll=2)
        copy = pltpu.make_async_copy(
            update.at[pl.ds(begin, rows)], update_hbm.at[pl.ds(begin, rows)], update_sems.at[chunk]
        )
        copy.start()
        update_copies.append(copy)

    wait_bytes(right_send.at[pl.ds(0, n - 1)], right_sems.at[0])
    wait_bytes(left_send.at[pl.ds(0, n - 1)], left_send_sems.at[0])
    for chunk in range(chunks):
        wait_bytes(mixed_send[chunk].at[pl.ds(0, n - 1)], mixed_send_sems.at[chunk])
        update_copies[chunk].wait()


def shards(
    pair,
    comp_len,
    tile_place,
    in_gain,
    in_bias,
    proj_weight,
    gate_weight,
    out_gain,
    out_bias,
    out_weight,
):
    tiles = tile_place.shape[0]
    side = pair.shape[1]
    width = pair.shape[3]
    channels = out_weight.shape[0]
    n = lax.axis_size("row")
    group = channels // n
    most_tiles = 2 + tiles // 16
    chunks = len(LEFT_PARTS)
    vmem = pl.BlockSpec(memory_space=pltpu.VMEM)
    smem = pl.BlockSpec(memory_space=pltpu.SMEM)
    hbm = pl.BlockSpec(memory_space=pl.ANY)
    by_part = [pltpu.VMEM((n, group, rows, side), jnp.bfloat16) for rows in LEFT_PARTS]
    result = pl.pallas_call(
        functools.partial(kernel, n, most_tiles),
        out_shape=jax.ShapeDtypeStruct((side, side, width), jnp.bfloat16),
        in_specs=[smem] * 2 + [hbm] + [vmem] * 7,
        out_specs=hbm,
        scratch_shapes=[
            pltpu.SMEM((n * most_tiles,), jnp.int32),
            pltpu.SMEM((n * most_tiles,), jnp.int32),
            pltpu.SMEM((n * most_tiles,), jnp.float32),
            pltpu.VMEM((side, side, width), jnp.bfloat16),
            pltpu.VMEM((side, side, width), jnp.bfloat16),
            pltpu.VMEM((4 * channels, width), jnp.bfloat16),
            pltpu.VMEM((channels, side), jnp.float32),
            pltpu.VMEM((channels, side), jnp.float32),
            pltpu.VMEM((channels * max(RIGHT_PARTS + LEFT_PARTS), side), jnp.float32),
            pltpu.VMEM((n, group, side, side), jnp.bfloat16),
            pltpu.VMEM((n, group, side, side), jnp.bfloat16),
            pltpu.VMEM((n, group, side, side), jnp.bfloat16),
            pltpu.SemaphoreType.DMA((2,)),
            pltpu.SemaphoreType.DMA((1,)),
            pltpu.SemaphoreType.DMA((chunks,)),
            pltpu.SemaphoreType.DMA((chunks,)),
            pltpu.SemaphoreType.DMA((chunks,)),
            pltpu.SemaphoreType.DMA((1 + 2 * chunks,)),
            pltpu.SemaphoreType.DMA((len(RIGHT_PARTS),)),
            pltpu.SemaphoreType.DMA((chunks,)),
        ]
        + by_part * 3,
        compiler_params=pltpu.CompilerParams(
            collective_id=0, has_side_effects=True, vmem_limit_bytes=56 * 1024 * 1024
        ),
    )(
        comp_len,
        tile_place,
        pair[0],
        in_gain[None, :],
        in_bias[None, :],
        proj_weight,
        gate_weight,
        out_gain[None, :],
        out_bias[None, :],
        out_weight,
    )
    return result[None]


def solution(mesh):
    placed = (
        P(("groups", "row"), None, None, None),
        P("groups"),
        P("groups"),
        P(),
        P(),
        P(),
        P(),
        P(),
        P(),
        P(),
    )
    return jax.shard_map(
        shards,
        mesh=mesh,
        in_specs=placed,
        out_specs=P(("groups", "row"), None, None, None),
        check_vma=False,
    )
```

```python
import functools
import jax
import jax.numpy as jnp
from jax import lax
from jax.experimental import pallas as pl
from jax.experimental.pallas import tpu as pltpu
from jax.sharding import PartitionSpec as P

RIGHT_PARTS = (16, 16, 32, 64)
LEFT_PARTS = (32, 32, 32, 16, 16)
UNROLL = 4


def spans(parts):
    first = 0
    for rows in parts:
        yield (first, rows)
        first += rows


def normalize_row(values, gain, offset):
    values = values.astype(jnp.float32)
    average = jnp.mean(values, 1, keepdims=True)
    centred = values - average
    variance = jnp.mean(centred * centred, 1, keepdims=True)
    scaled = centred * lax.rsqrt(variance + 1e-05)
    return (scaled * gain + offset).astype(jnp.bfloat16)


def unpack_mixed(mixed, stage, rows):
    sources, group = mixed.shape[:2]

    def unpack(source, carry):
        for g in range(group):
            first = pl.multiple_of((source * group + g) * rows, rows)
            stage[pl.ds(first, rows), :] = mixed[source, g].astype(jnp.float32)
        return carry

    lax.fori_loop(0, sources, unpack, 0)


def finish_row(values, gain_cols, bias_cols, out_weight, normed, gate_weight):
    average = jnp.mean(values, 0, keepdims=True)
    centred = values - average
    variance = jnp.mean(centred * centred, 0, keepdims=True)
    scaled = centred * lax.rsqrt(variance + 1e-05)
    mixed_norm = (scaled * gain_cols + bias_cols).T.astype(jnp.bfloat16)
    projected = jnp.dot(mixed_norm, out_weight, preferred_element_type=jnp.float32)
    gating = jax.nn.sigmoid(jnp.dot(normed, gate_weight, preferred_element_type=jnp.float32))
    return (gating * projected).astype(jnp.bfloat16)


def finish_kernel(
    partial,
    mixed,
    pair,
    in_gain,
    in_bias,
    gate_weight,
    out_gain,
    out_bias,
    out_weight,
    update,
    gain_cols,
    bias_cols,
    stage,
    last,
    sems,
):
    side = partial.shape[0]
    channels = out_weight.shape[0]
    rows = last.shape[0]
    copies = []
    for index in range(side // rows - 1):
        span = pl.ds(index * rows, rows)
        copies.append(pltpu.make_async_copy(partial.at[span], update.at[span], sems.at[index]))
        copies[-1].start()
    gain_cols[...] = jnp.broadcast_to(out_gain[...], (side, channels)).T
    bias_cols[...] = jnp.broadcast_to(out_bias[...], (side, channels)).T
    unpack_mixed(mixed, stage, rows)

    def finish(row, carry):
        last[row] = finish_row(
            stage[pl.ds(row, channels, stride=rows), :],
            gain_cols[...],
            bias_cols[...],
            out_weight[...],
            normalize_row(pair[row], in_gain[...], in_bias[...]),
            gate_weight[...],
        )
        return carry

    lax.fori_loop(0, rows, finish, 0, unroll=UNROLL)
    copy = pltpu.make_async_copy(
        last, update.at[pl.ds(side - rows, rows)], sems.at[side // rows - 1]
    )
    copy.start()
    for other in copies:
        other.wait()
    copy.wait()


def kernel(
    n,
    most_tiles,
    comp_len,
    tile_place,
    pair_hbm,
    in_gain,
    in_bias,
    proj_weight,
    gate_weight,
    out_gain,
    out_bias,
    out_weight,
    update_hbm,
    mixed_last,
    left_slot,
    right_slot,
    valid,
    pair,
    update,
    weights_t,
    gain_cols,
    bias_cols,
    stage,
    right_send,
    right_recv,
    left_send,
    right_sems,
    left_send_sems,
    left_recv_sems,
    mixed_send_sems,
    mixed_recv_sems,
    own_sems,
    pair_sems,
    update_sems,
    *parts,
):
    chunks = len(LEFT_PARTS)
    left_recv = parts[:chunks]
    mixed_send = parts[chunks : 2 * chunks]
    mixed_recv = parts[2 * chunks :]
    side = pair.shape[0]
    channels = out_weight.shape[0]
    group = channels // n
    me = lax.axis_index("row")

    pair_copies = []
    for index, (first, rows) in enumerate(spans(RIGHT_PARTS)):
        copy = pltpu.make_async_copy(
            pair_hbm.at[pl.ds(first, rows)], pair.at[pl.ds(first, rows)], pair_sems.at[index]
        )
        copy.start()
        pair_copies.append(copy)

    barrier = pltpu.get_barrier_semaphore()

    @pl.loop(1, n)
    def _(step):
        peer = lax.rem(me + step, n)
        pl.semaphore_signal(
            barrier, inc=1, device_id={"row": peer}, device_id_type=pl.DeviceIdType.MESH
        )

    def peer_at(position):
        half = position // 2
        step = jnp.where(position % 2 == 0, n // 2 + half, half + 1)
        return lax.rem(me + step, n)

    def describe(slot):
        number = lax.fori_loop(
            0, n, lambda t, found: found + jnp.where(tile_place[t] == slot, t, 0), 0, unroll=4
        )
        start, first, count_in, length = 0, 0, 0, 0
        for c in range(comp_len.shape[0]):
            count = lax.div(comp_len[c] + (side - 1), side)
            inside = (number >= start) & (number < start + count * count)
            first = jnp.where(inside, start, first)
            count_in = jnp.where(inside, count, count_in)
            length = jnp.where(inside, comp_len[c], length)
            start = start + count * count
        local = number - first
        row = 0
        for m in range(1, most_tiles):
            row = row + jnp.where(local >= m * count_in, 1, 0)
        return first, count_in, length, row, local - row * count_in

    _, _, own_length, own_row, own_col = describe(me)
    rows_left = own_length - own_row * side
    cols_left = own_length - own_col * side

    weights_t[...] = proj_weight[...].astype(jnp.float32).T.astype(jnp.bfloat16)

    def normalize(row):
        return normalize_row(pair[row], in_gain[...], in_bias[...])

    def project(which, begin, rows, send):
        cols = lax.broadcasted_iota(jnp.int32, (1, side), 1)
        cols_ok = (cols < cols_left).astype(jnp.float32)

        def one_row(row, carry):
            normed = normalize(begin + row)
            projected = lax.dot_general(
                weights_t[pl.ds(2 * which * channels, 2 * channels), :],
                normed,
                (((1,), (1,)), ((), ())),
                preferred_element_type=jnp.float32,
            )
            row_ok = (begin + row < rows_left).astype(jnp.float32)
            result = cols_ok * row_ok * jax.nn.sigmoid(projected[:channels]) * projected[channels:]
            stage[pl.ds(row, channels, stride=rows), :] = result
            return carry

        lax.fori_loop(0, rows, one_row, 0, unroll=UNROLL)

        def one_peer(peer, carry):
            for g in range(group):
                first = pl.multiple_of((peer * group + g) * rows, rows)
                send[peer, g, pl.ds(begin, rows), :] = stage[pl.ds(first, rows), :].astype(
                    jnp.bfloat16
                )
            return carry

        lax.fori_loop(0, n, one_peer, 0)

    def remote(src, dst, send_sem, recv_sem, peer):
        return pltpu.make_async_remote_copy(
            src_ref=src,
            dst_ref=dst,
            send_sem=send_sem,
            recv_sem=recv_sem,
            device_id={"row": peer},
            device_id_type=pl.DeviceIdType.MESH,
        )

    def wait_bytes(ref, sem):
        pltpu.make_async_copy(ref, ref, sem).wait()

    for index, (begin, rows) in enumerate(spans(RIGHT_PARTS)):
        pair_copies[index].wait()
        project(1, begin, rows, right_send)
        if index == 0:
            pl.semaphore_wait(barrier, n - 1)

        @pl.loop(0, n - 1)
        def _(position):
            peer = peer_at(position)
            remote(
                right_send.at[peer, :, pl.ds(begin, rows), :],
                right_recv.at[me, :, pl.ds(begin, rows), :],
                right_sems.at[0],
                right_sems.at[1],
                peer,
            ).start()

    own_right = pltpu.make_async_copy(right_send.at[me], right_recv.at[me], own_sems.at[0])
    own_right.start()

    own_left = []
    for chunk, (begin, rows) in enumerate(spans(LEFT_PARTS)):
        project(0, begin, rows, left_send)

        @pl.loop(0, n - 1)
        def _(position):
            peer = peer_at(position)
            remote(
                left_send.at[peer, :, pl.ds(begin, rows), :],
                left_recv[chunk].at[me],
                left_send_sems.at[0],
                left_recv_sems.at[chunk],
                peer,
            ).start()

        copy = pltpu.make_async_copy(
            left_send.at[me, :, pl.ds(begin, rows), :],
            left_recv[chunk].at[me],
            own_sems.at[1 + chunk],
        )
        copy.start()
        own_left.append(copy)

    gain_cols[...] = jnp.broadcast_to(out_gain[...], (side, channels)).T
    bias_cols[...] = jnp.broadcast_to(out_bias[...], (side, channels)).T

    @pl.loop(0, n)
    def _(slot):
        first, count, _, row, col = describe(slot)
        for k in range(most_tiles):
            entry = slot * most_tiles + k
            left_slot[entry] = tile_place[jnp.clip(first + row * count + k, 0, n - 1)]
            right_slot[entry] = tile_place[jnp.clip(first + col * count + k, 0, n - 1)]
            valid[entry] = (k < count).astype(jnp.float32)

    own_right.wait()
    wait_bytes(right_recv.at[pl.ds(0, n - 1)], right_sems.at[1])

    own_mixed = []
    for chunk, (begin, rows) in enumerate(spans(LEFT_PARTS)):
        own_left[chunk].wait()
        wait_bytes(left_recv[chunk].at[pl.ds(0, n - 1)], left_recv_sems.at[chunk])

        def product(tile):
            for g in range(group):
                total = jnp.zeros((rows, side), jnp.float32)
                for k in range(most_tiles):
                    entry = tile * most_tiles + k
                    part = lax.dot_general(
                        left_recv[chunk][left_slot[entry], g],
                        right_recv[right_slot[entry], g],
                        (((1,), (1,)), ((), ())),
                        preferred_element_type=jnp.float32,
                    )
                    total = total + part * valid[entry]
                mixed_send[chunk][tile, g] = total.astype(jnp.bfloat16)

        @pl.loop(0, n - 1)
        def _(position):
            tile = peer_at(position)
            product(tile)
            remote(
                mixed_send[chunk].at[tile],
                mixed_recv[chunk].at[me],
                mixed_send_sems.at[chunk],
                mixed_recv_sems.at[chunk],
                tile,
            ).start()

        product(me)
        copy = pltpu.make_async_copy(
            mixed_send[chunk].at[me], mixed_recv[chunk].at[me], own_sems.at[1 + chunks + chunk]
        )
        copy.start()
        own_mixed.append(copy)

    update_copies = []
    for chunk, (begin, rows) in enumerate(spans(LEFT_PARTS)):
        own_mixed[chunk].wait()
        wait_bytes(mixed_recv[chunk].at[pl.ds(0, n - 1)], mixed_recv_sems.at[chunk])

        if chunk == chunks - 1:
            copy = pltpu.make_async_copy(mixed_recv[chunk], mixed_last, update_sems.at[chunk])
            copy.start()
            update_copies.append(copy)
            continue

        unpack_mixed(mixed_recv[chunk], stage, rows)

        def finish(row, carry):
            update[begin + row] = finish_row(
                stage[pl.ds(row, channels, stride=rows), :],
                gain_cols[...],
                bias_cols[...],
                out_weight[...],
                normalize(begin + row),
                gate_weight[...],
            )
            return carry

        lax.fori_loop(0, rows, finish, 0, unroll=UNROLL)
        copy = pltpu.make_async_copy(
            update.at[pl.ds(begin, rows)], update_hbm.at[pl.ds(begin, rows)], update_sems.at[chunk]
        )
        copy.start()
        update_copies.append(copy)

    wait_bytes(right_send.at[pl.ds(0, n - 1)], right_sems.at[0])
    wait_bytes(left_send.at[pl.ds(0, n - 1)], left_send_sems.at[0])
    for chunk in range(chunks):
        wait_bytes(mixed_send[chunk].at[pl.ds(0, n - 1)], mixed_send_sems.at[chunk])
        update_copies[chunk].wait()


def shards(
    pair,
    comp_len,
    tile_place,
    in_gain,
    in_bias,
    proj_weight,
    gate_weight,
    out_gain,
    out_bias,
    out_weight,
):
    tiles = tile_place.shape[0]
    side = pair.shape[1]
    width = pair.shape[3]
    channels = out_weight.shape[0]
    n = lax.axis_size("row")
    group = channels // n
    most_tiles = 2 + tiles // 16
    chunks = len(LEFT_PARTS)
    vmem = pl.BlockSpec(memory_space=pltpu.VMEM)
    smem = pl.BlockSpec(memory_space=pltpu.SMEM)
    hbm = pl.BlockSpec(memory_space=pl.ANY)
    by_part = [pltpu.VMEM((n, group, rows, side), jnp.bfloat16) for rows in LEFT_PARTS]
    last = LEFT_PARTS[-1]
    partial, mixed_last = pl.pallas_call(
        functools.partial(kernel, n, most_tiles),
        out_shape=(
            jax.ShapeDtypeStruct((side, side, width), jnp.bfloat16),
            jax.ShapeDtypeStruct((n, group, last, side), jnp.bfloat16),
        ),
        in_specs=[smem] * 2 + [hbm] + [vmem] * 7,
        out_specs=(hbm, hbm),
        scratch_shapes=[
            pltpu.SMEM((n * most_tiles,), jnp.int32),
            pltpu.SMEM((n * most_tiles,), jnp.int32),
            pltpu.SMEM((n * most_tiles,), jnp.float32),
            pltpu.VMEM((side, side, width), jnp.bfloat16),
            pltpu.VMEM((side, side, width), jnp.bfloat16),
            pltpu.VMEM((4 * channels, width), jnp.bfloat16),
            pltpu.VMEM((channels, side), jnp.float32),
            pltpu.VMEM((channels, side), jnp.float32),
            pltpu.VMEM((channels * max(RIGHT_PARTS + LEFT_PARTS), side), jnp.float32),
            pltpu.VMEM((n, group, side, side), jnp.bfloat16),
            pltpu.VMEM((n, group, side, side), jnp.bfloat16),
            pltpu.VMEM((n, group, side, side), jnp.bfloat16),
            pltpu.SemaphoreType.DMA((2,)),
            pltpu.SemaphoreType.DMA((1,)),
            pltpu.SemaphoreType.DMA((chunks,)),
            pltpu.SemaphoreType.DMA((chunks,)),
            pltpu.SemaphoreType.DMA((chunks,)),
            pltpu.SemaphoreType.DMA((1 + 2 * chunks,)),
            pltpu.SemaphoreType.DMA((len(RIGHT_PARTS),)),
            pltpu.SemaphoreType.DMA((chunks,)),
        ]
        + by_part * 3,
        compiler_params=pltpu.CompilerParams(
            collective_id=0, has_side_effects=True, vmem_limit_bytes=56 * 1024 * 1024
        ),
    )(
        comp_len,
        tile_place,
        pair[0],
        in_gain[None, :],
        in_bias[None, :],
        proj_weight,
        gate_weight,
        out_gain[None, :],
        out_bias[None, :],
        out_weight,
    )
    result = pl.pallas_call(
        finish_kernel,
        grid=(1,),
        out_shape=jax.ShapeDtypeStruct((side, side, width), jnp.bfloat16),
        in_specs=[
            hbm,
            vmem,
            pl.BlockSpec((last, side, width), lambda step: (side // last - 1, 0, 0)),
        ]
        + [vmem] * 6,
        out_specs=hbm,
        scratch_shapes=[
            pltpu.VMEM((channels, side), jnp.float32),
            pltpu.VMEM((channels, side), jnp.float32),
            pltpu.VMEM((channels * last, side), jnp.float32),
            pltpu.VMEM((last, side, width), jnp.bfloat16),
            pltpu.SemaphoreType.DMA((side // last,)),
        ],
        compiler_params=pltpu.CompilerParams(vmem_limit_bytes=32 * 1024 * 1024),
    )(
        partial,
        mixed_last,
        pair[0],
        in_gain[None, :],
        in_bias[None, :],
        gate_weight,
        out_gain[None, :],
        out_bias[None, :],
        out_weight,
    )
    return result[None]


def solution(mesh):
    placed = (
        P(("groups", "row"), None, None, None),
        P("groups"),
        P("groups"),
        P(),
        P(),
        P(),
        P(),
        P(),
        P(),
        P(),
    )
    return jax.shard_map(
        shards,
        mesh=mesh,
        in_specs=placed,
        out_specs=P(("groups", "row"), None, None, None),
        check_vma=False,
    )
```

```python
import functools
import jax
import jax.numpy as jnp
from jax import lax
from jax.experimental import pallas as pl
from jax.experimental.pallas import tpu as pltpu
from jax.sharding import PartitionSpec as P

RIGHT_PARTS = (16, 16, 32, 64)
LEFT_PARTS = (32, 32, 32, 16, 16)
UNROLL = 4


def spans(parts):
    first = 0
    for rows in parts:
        yield (first, rows)
        first += rows


def normalize_row(values, gain, offset):
    values = values.astype(jnp.float32)
    average = jnp.mean(values, 1, keepdims=True)
    centred = values - average
    variance = jnp.mean(centred * centred, 1, keepdims=True)
    scaled = centred * lax.rsqrt(variance + 1e-05)
    return (scaled * gain + offset).astype(jnp.bfloat16)


def unpack_mixed(mixed, stage, rows):
    sources, group = mixed.shape[:2]

    def unpack(source, carry):
        for g in range(group):
            first = pl.multiple_of((source * group + g) * rows, rows)
            stage[pl.ds(first, rows), :] = mixed[source, g].astype(jnp.float32)
        return carry

    lax.fori_loop(0, sources, unpack, 0)


def finish_row(values, gain_cols, bias_cols, out_weight, normed, gate_weight):
    average = jnp.mean(values, 0, keepdims=True)
    centred = values - average
    variance = jnp.mean(centred * centred, 0, keepdims=True)
    scaled = centred * lax.rsqrt(variance + 1e-05)
    mixed_norm = (scaled * gain_cols + bias_cols).T.astype(jnp.bfloat16)
    projected = jnp.dot(mixed_norm, out_weight, preferred_element_type=jnp.float32)
    gating = jax.nn.sigmoid(jnp.dot(normed, gate_weight, preferred_element_type=jnp.float32))
    return (gating * projected).astype(jnp.bfloat16)


def finish_kernel(
    partial,
    mixed,
    pair,
    in_gain,
    in_bias,
    gate_weight,
    out_gain,
    out_bias,
    out_weight,
    update,
    gain_cols,
    bias_cols,
    stage,
    last,
    held,
    sems,
    held_sems,
):
    side = partial.shape[0]
    channels = out_weight.shape[0]
    rows = last.shape[0]
    copies = []
    for index in range(side // rows - 1):
        span = pl.ds(index * rows, rows)
        copies.append(
            (
                pltpu.make_async_copy(partial.at[span], held.at[span], held_sems.at[index]),
                pltpu.make_async_copy(held.at[span], update.at[span], sems.at[index]),
            )
        )
        copies[-1][0].start()
    gain_cols[...] = jnp.broadcast_to(out_gain[...], (side, channels)).T
    bias_cols[...] = jnp.broadcast_to(out_bias[...], (side, channels)).T
    unpack_mixed(mixed, stage, rows)
    for fetch, store in copies:
        fetch.wait()
        store.start()

    def finish(row, carry):
        last[row] = finish_row(
            stage[pl.ds(row, channels, stride=rows), :],
            gain_cols[...],
            bias_cols[...],
            out_weight[...],
            normalize_row(pair[row], in_gain[...], in_bias[...]),
            gate_weight[...],
        )
        return carry

    lax.fori_loop(0, rows, finish, 0, unroll=UNROLL)
    copy = pltpu.make_async_copy(
        last, update.at[pl.ds(side - rows, rows)], sems.at[side // rows - 1]
    )
    copy.start()
    for _, store in copies:
        store.wait()
    copy.wait()


def kernel(
    n,
    most_tiles,
    comp_len,
    tile_place,
    pair_hbm,
    in_gain,
    in_bias,
    proj_weight,
    gate_weight,
    out_gain,
    out_bias,
    out_weight,
    update_hbm,
    mixed_last,
    left_slot,
    right_slot,
    valid,
    pair,
    update,
    weights_t,
    gain_cols,
    bias_cols,
    stage,
    right_send,
    right_recv,
    left_send,
    right_sems,
    left_send_sems,
    left_recv_sems,
    mixed_send_sems,
    mixed_recv_sems,
    own_sems,
    pair_sems,
    update_sems,
    *parts,
):
    chunks = len(LEFT_PARTS)
    left_recv = parts[:chunks]
    mixed_send = parts[chunks : 2 * chunks]
    mixed_recv = parts[2 * chunks :]
    side = pair.shape[0]
    channels = out_weight.shape[0]
    group = channels // n
    me = lax.axis_index("row")

    pair_copies = []
    for index, (first, rows) in enumerate(spans(RIGHT_PARTS)):
        copy = pltpu.make_async_copy(
            pair_hbm.at[pl.ds(first, rows)], pair.at[pl.ds(first, rows)], pair_sems.at[index]
        )
        copy.start()
        pair_copies.append(copy)

    barrier = pltpu.get_barrier_semaphore()

    @pl.loop(1, n)
    def _(step):
        peer = lax.rem(me + step, n)
        pl.semaphore_signal(
            barrier, inc=1, device_id={"row": peer}, device_id_type=pl.DeviceIdType.MESH
        )

    def peer_at(position):
        half = position // 2
        step = jnp.where(position % 2 == 0, n // 2 + half, half + 1)
        return lax.rem(me + step, n)

    def describe(slot):
        number = lax.fori_loop(
            0, n, lambda t, found: found + jnp.where(tile_place[t] == slot, t, 0), 0, unroll=4
        )
        start, first, count_in, length = 0, 0, 0, 0
        for c in range(comp_len.shape[0]):
            count = lax.div(comp_len[c] + (side - 1), side)
            inside = (number >= start) & (number < start + count * count)
            first = jnp.where(inside, start, first)
            count_in = jnp.where(inside, count, count_in)
            length = jnp.where(inside, comp_len[c], length)
            start = start + count * count
        local = number - first
        row = 0
        for m in range(1, most_tiles):
            row = row + jnp.where(local >= m * count_in, 1, 0)
        return first, count_in, length, row, local - row * count_in

    _, _, own_length, own_row, own_col = describe(me)
    rows_left = own_length - own_row * side
    cols_left = own_length - own_col * side

    weights_t[...] = proj_weight[...].astype(jnp.float32).T.astype(jnp.bfloat16)

    def normalize(row):
        return normalize_row(pair[row], in_gain[...], in_bias[...])

    def project(which, begin, rows, send):
        cols = lax.broadcasted_iota(jnp.int32, (1, side), 1)
        cols_ok = (cols < cols_left).astype(jnp.float32)

        def one_row(row, carry):
            normed = normalize(begin + row)
            projected = lax.dot_general(
                weights_t[pl.ds(2 * which * channels, 2 * channels), :],
                normed,
                (((1,), (1,)), ((), ())),
                preferred_element_type=jnp.float32,
            )
            row_ok = (begin + row < rows_left).astype(jnp.float32)
            result = cols_ok * row_ok * jax.nn.sigmoid(projected[:channels]) * projected[channels:]
            stage[pl.ds(row, channels, stride=rows), :] = result
            return carry

        lax.fori_loop(0, rows, one_row, 0, unroll=UNROLL)

        def one_peer(peer, carry):
            for g in range(group):
                first = pl.multiple_of((peer * group + g) * rows, rows)
                send[peer, g, pl.ds(begin, rows), :] = stage[pl.ds(first, rows), :].astype(
                    jnp.bfloat16
                )
            return carry

        lax.fori_loop(0, n, one_peer, 0)

    def remote(src, dst, send_sem, recv_sem, peer):
        return pltpu.make_async_remote_copy(
            src_ref=src,
            dst_ref=dst,
            send_sem=send_sem,
            recv_sem=recv_sem,
            device_id={"row": peer},
            device_id_type=pl.DeviceIdType.MESH,
        )

    def wait_bytes(ref, sem):
        pltpu.make_async_copy(ref, ref, sem).wait()

    for index, (begin, rows) in enumerate(spans(RIGHT_PARTS)):
        pair_copies[index].wait()
        project(1, begin, rows, right_send)
        if index == 0:
            pl.semaphore_wait(barrier, n - 1)

        @pl.loop(0, n - 1)
        def _(position):
            peer = peer_at(position)
            remote(
                right_send.at[peer, :, pl.ds(begin, rows), :],
                right_recv.at[me, :, pl.ds(begin, rows), :],
                right_sems.at[0],
                right_sems.at[1],
                peer,
            ).start()

    own_right = pltpu.make_async_copy(right_send.at[me], right_recv.at[me], own_sems.at[0])
    own_right.start()

    own_left = []
    for chunk, (begin, rows) in enumerate(spans(LEFT_PARTS)):
        project(0, begin, rows, left_send)

        @pl.loop(0, n - 1)
        def _(position):
            peer = peer_at(position)
            remote(
                left_send.at[peer, :, pl.ds(begin, rows), :],
                left_recv[chunk].at[me],
                left_send_sems.at[0],
                left_recv_sems.at[chunk],
                peer,
            ).start()

        copy = pltpu.make_async_copy(
            left_send.at[me, :, pl.ds(begin, rows), :],
            left_recv[chunk].at[me],
            own_sems.at[1 + chunk],
        )
        copy.start()
        own_left.append(copy)

    gain_cols[...] = jnp.broadcast_to(out_gain[...], (side, channels)).T
    bias_cols[...] = jnp.broadcast_to(out_bias[...], (side, channels)).T

    @pl.loop(0, n)
    def _(slot):
        first, count, _, row, col = describe(slot)
        for k in range(most_tiles):
            entry = slot * most_tiles + k
            left_slot[entry] = tile_place[jnp.clip(first + row * count + k, 0, n - 1)]
            right_slot[entry] = tile_place[jnp.clip(first + col * count + k, 0, n - 1)]
            valid[entry] = (k < count).astype(jnp.float32)

    own_right.wait()
    wait_bytes(right_recv.at[pl.ds(0, n - 1)], right_sems.at[1])

    own_mixed = []
    for chunk, (begin, rows) in enumerate(spans(LEFT_PARTS)):
        own_left[chunk].wait()
        wait_bytes(left_recv[chunk].at[pl.ds(0, n - 1)], left_recv_sems.at[chunk])

        def product(tile):
            for g in range(group):
                total = jnp.zeros((rows, side), jnp.float32)
                for k in range(most_tiles):
                    entry = tile * most_tiles + k
                    part = lax.dot_general(
                        left_recv[chunk][left_slot[entry], g],
                        right_recv[right_slot[entry], g],
                        (((1,), (1,)), ((), ())),
                        preferred_element_type=jnp.float32,
                    )
                    total = total + part * valid[entry]
                mixed_send[chunk][tile, g] = total.astype(jnp.bfloat16)

        @pl.loop(0, n - 1)
        def _(position):
            tile = peer_at(position)
            product(tile)
            remote(
                mixed_send[chunk].at[tile],
                mixed_recv[chunk].at[me],
                mixed_send_sems.at[chunk],
                mixed_recv_sems.at[chunk],
                tile,
            ).start()

        product(me)
        copy = pltpu.make_async_copy(
            mixed_send[chunk].at[me], mixed_recv[chunk].at[me], own_sems.at[1 + chunks + chunk]
        )
        copy.start()
        own_mixed.append(copy)

    update_copies = []
    for chunk, (begin, rows) in enumerate(spans(LEFT_PARTS)):
        own_mixed[chunk].wait()
        wait_bytes(mixed_recv[chunk].at[pl.ds(0, n - 1)], mixed_recv_sems.at[chunk])

        if chunk == chunks - 1:
            copy = pltpu.make_async_copy(mixed_recv[chunk], mixed_last, update_sems.at[chunk])
            copy.start()
            update_copies.append(copy)
            continue

        unpack_mixed(mixed_recv[chunk], stage, rows)

        def finish(row, carry):
            update[begin + row] = finish_row(
                stage[pl.ds(row, channels, stride=rows), :],
                gain_cols[...],
                bias_cols[...],
                out_weight[...],
                normalize(begin + row),
                gate_weight[...],
            )
            return carry

        lax.fori_loop(0, rows, finish, 0, unroll=UNROLL)
        copy = pltpu.make_async_copy(
            update.at[pl.ds(begin, rows)], update_hbm.at[pl.ds(begin, rows)], update_sems.at[chunk]
        )
        copy.start()
        update_copies.append(copy)

    wait_bytes(right_send.at[pl.ds(0, n - 1)], right_sems.at[0])
    wait_bytes(left_send.at[pl.ds(0, n - 1)], left_send_sems.at[0])
    for chunk in range(chunks):
        wait_bytes(mixed_send[chunk].at[pl.ds(0, n - 1)], mixed_send_sems.at[chunk])
        update_copies[chunk].wait()


def shards(
    pair,
    comp_len,
    tile_place,
    in_gain,
    in_bias,
    proj_weight,
    gate_weight,
    out_gain,
    out_bias,
    out_weight,
):
    tiles = tile_place.shape[0]
    side = pair.shape[1]
    width = pair.shape[3]
    channels = out_weight.shape[0]
    n = lax.axis_size("row")
    group = channels // n
    most_tiles = 2 + tiles // 16
    chunks = len(LEFT_PARTS)
    vmem = pl.BlockSpec(memory_space=pltpu.VMEM)
    smem = pl.BlockSpec(memory_space=pltpu.SMEM)
    hbm = pl.BlockSpec(memory_space=pl.ANY)
    by_part = [pltpu.VMEM((n, group, rows, side), jnp.bfloat16) for rows in LEFT_PARTS]
    last = LEFT_PARTS[-1]
    partial, mixed_last = pl.pallas_call(
        functools.partial(kernel, n, most_tiles),
        out_shape=(
            jax.ShapeDtypeStruct((side, side, width), jnp.bfloat16),
            jax.ShapeDtypeStruct((n, group, last, side), jnp.bfloat16),
        ),
        in_specs=[smem] * 2 + [hbm] + [vmem] * 7,
        out_specs=(hbm, hbm),
        scratch_shapes=[
            pltpu.SMEM((n * most_tiles,), jnp.int32),
            pltpu.SMEM((n * most_tiles,), jnp.int32),
            pltpu.SMEM((n * most_tiles,), jnp.float32),
            pltpu.VMEM((side, side, width), jnp.bfloat16),
            pltpu.VMEM((side, side, width), jnp.bfloat16),
            pltpu.VMEM((4 * channels, width), jnp.bfloat16),
            pltpu.VMEM((channels, side), jnp.float32),
            pltpu.VMEM((channels, side), jnp.float32),
            pltpu.VMEM((channels * max(RIGHT_PARTS + LEFT_PARTS), side), jnp.float32),
            pltpu.VMEM((n, group, side, side), jnp.bfloat16),
            pltpu.VMEM((n, group, side, side), jnp.bfloat16),
            pltpu.VMEM((n, group, side, side), jnp.bfloat16),
            pltpu.SemaphoreType.DMA((2,)),
            pltpu.SemaphoreType.DMA((1,)),
            pltpu.SemaphoreType.DMA((chunks,)),
            pltpu.SemaphoreType.DMA((chunks,)),
            pltpu.SemaphoreType.DMA((chunks,)),
            pltpu.SemaphoreType.DMA((1 + 2 * chunks,)),
            pltpu.SemaphoreType.DMA((len(RIGHT_PARTS),)),
            pltpu.SemaphoreType.DMA((chunks,)),
        ]
        + by_part * 3,
        compiler_params=pltpu.CompilerParams(
            collective_id=0, has_side_effects=True, vmem_limit_bytes=56 * 1024 * 1024
        ),
    )(
        comp_len,
        tile_place,
        pair[0],
        in_gain[None, :],
        in_bias[None, :],
        proj_weight,
        gate_weight,
        out_gain[None, :],
        out_bias[None, :],
        out_weight,
    )
    result = pl.pallas_call(
        finish_kernel,
        grid=(1,),
        out_shape=jax.ShapeDtypeStruct((side, side, width), jnp.bfloat16),
        in_specs=[
            hbm,
            vmem,
            pl.BlockSpec((last, side, width), lambda step: (side // last - 1, 0, 0)),
        ]
        + [vmem] * 6,
        out_specs=hbm,
        scratch_shapes=[
            pltpu.VMEM((channels, side), jnp.float32),
            pltpu.VMEM((channels, side), jnp.float32),
            pltpu.VMEM((channels * last, side), jnp.float32),
            pltpu.VMEM((last, side, width), jnp.bfloat16),
            pltpu.VMEM((side, side, width), jnp.bfloat16),
            pltpu.SemaphoreType.DMA((side // last,)),
            pltpu.SemaphoreType.DMA((side // last,)),
        ],
        compiler_params=pltpu.CompilerParams(vmem_limit_bytes=60 * 1024 * 1024),
    )(
        partial,
        mixed_last,
        pair[0],
        in_gain[None, :],
        in_bias[None, :],
        gate_weight,
        out_gain[None, :],
        out_bias[None, :],
        out_weight,
    )
    return result[None]


def solution(mesh):
    placed = (
        P(("groups", "row"), None, None, None),
        P("groups"),
        P("groups"),
        P(),
        P(),
        P(),
        P(),
        P(),
        P(),
        P(),
    )
    return jax.shard_map(
        shards,
        mesh=mesh,
        in_specs=placed,
        out_specs=P(("groups", "row"), None, None, None),
        check_vma=False,
    )
```
